256 devices in a mesh: cluster: 8 (over x, core), coupling: 32 (over z, y).
Axes of the slice: x: 4, y: 4, z: 8, core: 2. Of those that a mesh axis runs over, the one named last changes fastest.
Arguments:
- charges: bfloat16 [16384, 64, 64], P(('cluster', 'coupling')), may hold values from -6 to 6
- source_basis: bfloat16 [16384, 64, 64], P(('cluster', 'coupling')), may hold values from -0.75 to 0.75
- target_basis: bfloat16 [16384, 64, 64], P(('cluster', 'coupling')), may hold values from -0.75 to 0.75
- leaf_up: bfloat16 [16384, 64, 64], P(('cluster', 'coupling')), may hold values from -0.25 to 0.25
- mid_up: bfloat16 [2048, 64, 64], P(('cluster', 'coupling')), may hold values from -0.25 to 0.25
- leaf_down: bfloat16 [16384, 64, 64], P(('cluster', 'coupling')), may hold values from -0.75 to 0.75
- mid_down: bfloat16 [2048, 64, 64], P(('cluster', 'coupling')), may hold values from -0.75 to 0.75
- leaf_far_src: int32 [16384, 8], P(('cluster', 'coupling')), may hold values from 0 to 16383, as said below
- leaf_far_mat: bfloat16 [16384, 8, 64, 64], P(('cluster', 'coupling')), may hold values from -0.25 to 0.25
- mid_far_src: int32 [2048, 16], P(('cluster', 'coupling')), may hold values from 0 to 2047, as said below
- mid_far_mat: bfloat16 [2048, 16, 64, 64], P(('cluster', 'coupling')), may hold values from -0.1875 to 0.1875
- top_far_src: int32 [256, 32], P(('cluster', 'coupling')), may hold values from 0 to 255
- top_far_mat: bfloat16 [256, 32, 64, 64], P(('cluster', 'coupling')), may hold values from -0.125 to 0.125
- near_src: int32 [16384, 8], P(('cluster', 'coupling')), may hold values from 0 to 16383, as said below
- near_count: int32 [16384], P(('cluster', 'coupling')), may hold values from 1 to 8, as said below
- near_mat: bfloat16 [16384, 8, 64, 64], P(('cluster', 'coupling')), may hold values from -0.25 to 0.25
Outputs:
- potential: bfloat16 [16384, 64, 64], P(('cluster', 'coupling'))
The draws below stay inside these ranges and needn't reach their ends.
Inputs may be any that keep to these rules, and one draw needn't show every extreme that they name: `leaf_far_src`: the sources of a leaf's coupling entries lie on the leaf's own device or on the devices just before or after it in the order cluster+coupling; entry 0 lies on the device before and entry 1 on the device after, where those exist. `near_src`: the sources of a leaf's near-field slots lie on the leaf's own device or on the devices just before or after it in the order cluster+coupling; slot 0 lies on the device before and slot 1 on the device after, where those exist. Only the first near_count[l] slots of leaf l are used. `mid_far_src`: the sources of a level-1 cluster p lie in its own block of 256 level-1 clusters, p // 256.
All inputs are finite; a program needn't handle non-finite values.
Results may differ from the reference program's by a relative error of at most 0.012.
Values may be sent and summed in bfloat16 or wider, within the bound.
No kernel may reach another device: no remote copies, remote signals or barrier semaphores. Data moves between devices by JAX's collectives and lax.ppermute only.
A program may use at most 128 MiB of HBM per device.

```python
import jax
import jax.numpy as jnp
from jax import lax

PTS = 64
RANK = 64
RHS = 64
LEAF_DEV = 64
NF0 = 8
NF1 = 16
NF2 = 32
NN = 8
LEAVES = 16384
C1 = 2048
C2 = 256
ROW_C1 = 256


def neighbour_leaves(key, count):
    first_key, second_key = jax.random.split(key)
    leaf = jnp.arange(LEAVES, dtype=jnp.int32)[:, None]
    device = leaf // LEAF_DEV
    steps = jax.random.randint(first_key, (LEAVES, count), -1, 2)
    steps = steps.at[:, 0].set(-1).at[:, 1].set(1)
    target = jnp.clip(device + steps, 0, LEAVES // LEAF_DEV - 1)
    within = jax.random.randint(second_key, (LEAVES, count), 0, LEAF_DEV)
    return (target * LEAF_DEV + within).astype(jnp.int32)


def draw_leaf_far_src(key, part):
    key = jax.random.fold_in(key, 11)
    return neighbour_leaves(key, NF0)


def draw_near_src(key, part):
    key = jax.random.fold_in(key, 13)
    return neighbour_leaves(key, NN)


def draw_near_count(key, part):
    key = jax.random.fold_in(key, 17)
    counts = jax.random.randint(key, (LEAVES,), 1, NN + 1)
    counts = counts.at[0::5].set(NN).at[1::5].set(1)
    return counts.astype(jnp.int32)


def draw_mid_far_src(key, part):
    key = jax.random.fold_in(key, 19)
    cluster = jnp.arange(C1, dtype=jnp.int32)[:, None]
    within = jax.random.randint(key, (C1, NF1), 0, ROW_C1)
    return (cluster // ROW_C1 * ROW_C1 + within).astype(jnp.int32)


def with_ends(entries, stream_key, least, high):
    longest = entries.shape.index(max(entries.shape))
    spots = []
    for shift in (0, 1):
        where = [jax.random.randint(jax.random.fold_in(stream_key, axis), (), 0, length) for axis, length in enumerate(entries.shape)]
        where[longest] = (where[longest] + shift) % entries.shape[longest]
        spots.append(tuple(where))
    return entries.at[spots[0]].set(least).at[spots[1]].set(high)


def block_levels(key, shape, cuts, least, largest):
    factor_of, own = 1.0, jax.random.fold_in(key, 6)
    for dim, blocks in cuts:
        steps = jnp.exp(jax.random.uniform(jax.random.fold_in(own, dim), (blocks,), jnp.float32, least / len(cuts), largest / len(cuts)))
        factor_of = factor_of * jnp.repeat(steps, shape[dim] // blocks).reshape([-1 if axis == dim else 1 for axis in range(len(shape))])
    return factor_of


def gaussian(key, dims, spread, most, pieces=(), held_as=jnp.bfloat16):
    loudness = block_levels(key, dims, pieces, -0.22, 0.18) if pieces else 1.0
    drawn = jax.random.normal(key, dims, jnp.float32) * spread * loudness
    return jnp.minimum(jnp.maximum(drawn, -most), most).astype(held_as)


def setup_inputs(seed: int = 0) -> dict:
    keys = jax.random.split(jax.random.key(seed), 17)
    charges = gaussian(keys[0], (LEAVES, PTS, RHS), 1.0, 6.0, ((0, 256),))
    source_basis = gaussian(keys[1], (LEAVES, PTS, RANK), PTS ** -0.5, 0.75, ((0, 256),))
    target_basis = gaussian(keys[2], (LEAVES, PTS, RANK), RANK ** -0.5, 0.75, ((0, 256),))
    leaf_up = gaussian(keys[3], (LEAVES, RANK, RANK), (8 * RANK) ** -0.5, 0.25, ((0, 256),))
    mid_up = gaussian(keys[4], (C1, RANK, RANK), (8 * RANK) ** -0.5, 0.25, ((0, 256),))
    leaf_down = gaussian(keys[5], (LEAVES, RANK, RANK), RANK ** -0.5, 0.75, ((0, 256),))
    mid_down = gaussian(keys[6], (C1, RANK, RANK), RANK ** -0.5, 0.75, ((0, 256),))
    leaf_far_src = draw_leaf_far_src(jax.random.fold_in(keys[16], 71), 0)
    leaf_far_mat = gaussian(keys[8], (LEAVES, NF0, RANK, RANK), (NF0 * RANK) ** -0.5, 0.25, ((0, 256),))
    mid_far_src = draw_mid_far_src(jax.random.fold_in(keys[16], 71), 0)
    mid_far_mat = gaussian(keys[10], (C1, NF1, RANK, RANK), (NF1 * RANK) ** -0.5, 0.1875, ((0, 256),))
    top_far_src = with_ends(jax.random.randint(keys[11], (C2, NF2), 0, C2), jax.random.fold_in(keys[11], 1), 0, C2 - 1).astype(jnp.int32)
    top_far_mat = gaussian(keys[12], (C2, NF2, RANK, RANK), (NF2 * RANK) ** -0.5, 0.125, ((0, 256),))
    near_src = draw_near_src(jax.random.fold_in(keys[16], 71), 0)
    near_count = draw_near_count(jax.random.fold_in(keys[16], 71), 0)
    near_mat = gaussian(keys[15], (LEAVES, NN, PTS, PTS), (NN * PTS) ** -0.5, 0.25, ((0, 256),))
    return dict(charges=charges, source_basis=source_basis, target_basis=target_basis, leaf_up=leaf_up, mid_up=mid_up, leaf_down=leaf_down, mid_down=mid_down, leaf_far_src=leaf_far_src, leaf_far_mat=leaf_far_mat, mid_far_src=mid_far_src, mid_far_mat=mid_far_mat, top_far_src=top_far_src, top_far_mat=top_far_mat, near_src=near_src, near_count=near_count, near_mat=near_mat)


def product(form, left, right):
    return jnp.einsum(form, left.astype(jnp.float32), right.astype(jnp.float32))


def reference(charges, source_basis, target_basis, leaf_up, mid_up, leaf_down, mid_down, leaf_far_src, leaf_far_mat, mid_far_src, mid_far_mat, top_far_src, top_far_mat, near_src, near_count, near_mat):
    leaf_coef = product("lpk,lpr->lkr", source_basis, charges).astype(jnp.bfloat16)
    mid_coef = product("lkj,lkr->ljr", leaf_up, leaf_coef).reshape(C1, 8, RANK, RHS).sum(axis=1).astype(jnp.bfloat16)
    top_coef = product("pkj,pkr->pjr", mid_up, mid_coef).reshape(C2, 8, RANK, RHS).sum(axis=1).astype(jnp.bfloat16)
    top_local = product("gnjk,gnkr->gjr", top_far_mat, top_coef[top_far_src]).astype(jnp.bfloat16)
    mid_far = product("pnjk,pnkr->pjr", mid_far_mat, mid_coef[mid_far_src])
    mid_local = (mid_far + product("pkj,pjr->pkr", mid_down, jnp.repeat(top_local, 8, axis=0))).astype(jnp.bfloat16)
    parent_local = jnp.repeat(mid_local, 8, axis=0)
    block = 512 if LEAVES % 512 == 0 else LEAVES

    def one_block(index):
        begin = index * block

        def cut(array):
            return lax.dynamic_slice_in_dim(array, begin, block, 0)

        far_sum = product("lnjk,lnkr->ljr", cut(leaf_far_mat), leaf_coef[cut(leaf_far_src)])
        local = (far_sum + product("lkj,ljr->lkr", cut(leaf_down), cut(parent_local))).astype(jnp.bfloat16)
        used = (jnp.arange(NN, dtype=jnp.int32)[None, :] < cut(near_count)[:, None]).astype(jnp.float32)
        picked = charges[cut(near_src)].astype(jnp.float32) * used[:, :, None, None]
        near_sum = jnp.einsum("lnpq,lnqr->lpr", cut(near_mat).astype(jnp.float32), picked)
        return (product("lpk,lkr->lpr", cut(target_basis), local) + near_sum).astype(jnp.bfloat16)

    result = lax.map(one_block, jnp.arange(LEAVES // block, dtype=jnp.int32))
    return result.reshape(LEAVES, PTS, RHS)
```

```python
import functools

import jax
import jax.numpy as jnp
from jax import lax
from jax.experimental import pallas as pl
from jax.experimental.pallas import tpu as pltpu
from jax.sharding import PartitionSpec as P

BOTH = ("cluster", "coupling")
X, CORE, Z, Y = 4, 2, 8, 4
R = 64
BF = jnp.bfloat16
F32 = jnp.float32
VMEM = pltpu.VMEM


def dot(a, b):
    return lax.dot_general(a, b, (((1,), (0,)), ((), ())), preferred_element_type=F32)


def dot_t(a, b):
    return lax.dot_general(a, b, (((0,), (0,)), ((), ())), preferred_element_type=F32)


def beside(a, b):
    return jnp.concatenate([a, b], axis=1)


def wide(blocks):
    return jnp.concatenate([beside(a, b) for a, b in zip(blocks[::2], blocks[1::2])], axis=1)


def up_kernel(c_ref, s_ref, lu_ref, mu_ref, pc_ref, pk_ref, mt_ref, acc):
    i = pl.program_id(0)

    @pl.when(i == 0)
    def _():
        acc[...] = jnp.zeros_like(acc)

    coefs = []
    for l in range(16):
        coefs.append(dot_t(s_ref[l], c_ref[l]).astype(BF))
    for j in range(8):
        pc_ref[j] = beside(c_ref[2 * j], c_ref[2 * j + 1])
        pk_ref[j] = beside(coefs[2 * j], coefs[2 * j + 1])
    mids = []
    for h in range(2):
        up = lu_ref[8 * h : 8 * h + 8].reshape(8 * R, R)
        mids.append(dot_t(up, jnp.concatenate(coefs[8 * h : 8 * h + 8], axis=0)).astype(BF))
    mt_ref[pl.ds(pl.multiple_of(i * R, R), R), :] = beside(*mids)
    acc[...] += dot_t(mu_ref[...].reshape(2 * R, R), jnp.concatenate(mids, axis=0))

    @pl.when(i == 3)
    def _():
        top = acc[...].astype(BF)
        mt_ref[256:288, :] = beside(top[:32], top[32:])


def upsweep(charges, source_basis, leaf_up, mid_up):
    leaf = pl.BlockSpec((16, R, R), lambda i: (i, 0, 0))
    pair = pl.BlockSpec((8, R, 2 * R), lambda i: (i, 0, 0))
    return pl.pallas_call(
        up_kernel,
        grid=(4,),
        in_specs=[leaf, leaf, leaf, pl.BlockSpec((2, R, R), lambda i: (i, 0, 0))],
        out_specs=[pair, pair, pl.BlockSpec((288, 128), lambda i: (0, 0))],
        out_shape=[
            jax.ShapeDtypeStruct((32, R, 2 * R), BF),
            jax.ShapeDtypeStruct((32, R, 2 * R), BF),
            jax.ShapeDtypeStruct((288, 128), BF),
        ],
        scratch_shapes=[VMEM((R, R), F32)],
        compiler_params=pltpu.CompilerParams(vmem_limit_bytes=16 << 20),
        cost_estimate=pl.CostEstimate(flops=136 * 2 * R**3, bytes_accessed=5 << 20, transcendentals=0),
        name="upsweep",
    )(charges, source_basis, leaf_up, mid_up)


def unpack(table, refs):
    def step(j, carry):
        for b, ref in enumerate(refs):
            x = ref[j]
            table[64 * b + 2 * j] = x[:, :R]
            table[64 * b + 2 * j + 1] = x[:, R:]
        return carry

    lax.fori_loop(0, 32, step, 0)


def near_kernel(info, src, cnt, bef, own, aft, mat, out, table):
    i = pl.program_id(0)

    @pl.when(i == 0)
    def _():
        unpack(table, (bef, own, aft))
        table[192] = jnp.zeros((R, R), BF)

    for j in range(8):
        l = i * 8 + j
        rows = []
        for n in range(8):
            k = jnp.clip(src[n, l] - info[0], 0, 191)
            rows.append(table[jnp.where(n < cnt[l], k, 192)])
        acc = dot(wide([mat[j, n] for n in range(4)]), jnp.concatenate(rows[:4], axis=0))
        out[j] = acc + dot(wide([mat[j, n] for n in range(4, 8)]), jnp.concatenate(rows[4:], axis=0))


def near_field(info, src, cnt, bef, own, aft, mat):
    whole = pl.BlockSpec((32, R, 2 * R), lambda i, *_: (0, 0, 0))
    return pl.pallas_call(
        near_kernel,
        grid_spec=pltpu.PrefetchScalarGridSpec(
            num_scalar_prefetch=3,
            grid=(8,),
            in_specs=[whole, whole, whole, pl.BlockSpec((8, 8, R, R), lambda i, *_: (i, 0, 0, 0))],
            out_specs=pl.BlockSpec((8, R, R), lambda i, *_: (i, 0, 0)),
            scratch_shapes=[VMEM((193, R, R), BF)],
        ),
        out_shape=jax.ShapeDtypeStruct((64, R, R), F32),
        compiler_params=pltpu.CompilerParams(vmem_limit_bytes=24 << 20),
        cost_estimate=pl.CostEstimate(flops=512 * 2 * R**3, bytes_accessed=12 << 20, transcendentals=0),
        name="near",
    )(info, src, cnt, bef, own, aft, mat)


def far_kernel(info, src, bef, own, aft, mat, tb, ld, near, base, both, table):
    i = pl.program_id(0)

    @pl.when(i == 0)
    def _():
        unpack(table, (bef, own, aft))

    for j in range(8):
        l = i * 8 + j
        rows = [table[jnp.clip(src[n, l] - info[0], 0, 191)] for n in range(8)]
        acc = dot(wide([mat[j, n] for n in range(4)]), jnp.concatenate(rows[:4], axis=0))
        acc += dot(wide([mat[j, n] for n in range(4, 8)]), jnp.concatenate(rows[4:], axis=0))
        t = tb[j]
        base[j] = near[j] + dot(t, acc.astype(BF))
        both[j] = dot(t, ld[j]).astype(BF)


def leaf_far(info, src, bef, own, aft, mat, tb, ld, near):
    whole = pl.BlockSpec((32, R, 2 * R), lambda i, *_: (0, 0, 0))
    leaf = pl.BlockSpec((8, R, R), lambda i, *_: (i, 0, 0))
    return pl.pallas_call(
        far_kernel,
        grid_spec=pltpu.PrefetchScalarGridSpec(
            num_scalar_prefetch=2,
            grid=(8,),
            in_specs=[whole, whole, whole, pl.BlockSpec((8, 8, R, R), lambda i, *_: (i, 0, 0, 0)), leaf, leaf, leaf],
            out_specs=[leaf, leaf],
            scratch_shapes=[VMEM((192, R, R), BF)],
        ),
        out_shape=[jax.ShapeDtypeStruct((64, R, R), F32), jax.ShapeDtypeStruct((64, R, R), BF)],
        compiler_params=pltpu.CompilerParams(vmem_limit_bytes=24 << 20),
        cost_estimate=pl.CostEstimate(flops=640 * 2 * R**3, bytes_accessed=16 << 20, transcendentals=0),
        name="leaf_far",
    )(info, src, bef, own, aft, mat, tb, ld, near)


def top_kernel(info, src, own, other, mat, out):
    x, core, z, y = info[1], info[2], info[3], info[4]
    acc = jnp.zeros((R, R), F32)
    rows = []
    for n in range(32):
        g = jnp.clip(src[0, n], 0, X * CORE * Z * Y - 1)
        sy = lax.rem(y - lax.rem(g, Y) + Y, Y)
        sz = lax.rem(z - lax.rem(g // Y, Z) + Z, Z)
        sx = lax.rem(x - g // (CORE * Z * Y) + X, X)
        same = lax.rem(g // (Z * Y), CORE) == core
        at = pl.ds(pl.multiple_of(((sx * Z + sz) * Y + sy) * 32, 32), 32)
        t = jnp.where(same, own[at, :], other[at, :])
        rows += [t[:, :R], t[:, R:]]
    for q in range(8):
        acc += dot(wide([mat[0, 4 * q + n] for n in range(4)]), jnp.concatenate(rows[8 * q : 8 * q + 8], axis=0))
    out[...] = acc.astype(BF)


def top_far(info, src, own, other, mat):
    v = pl.BlockSpec(memory_space=VMEM)
    s = pl.BlockSpec(memory_space=pltpu.SMEM)
    return pl.pallas_call(
        top_kernel,
        in_specs=[s, s, v, v, v],
        out_specs=v,
        out_shape=jax.ShapeDtypeStruct((R, R), BF),
        compiler_params=pltpu.CompilerParams(vmem_limit_bytes=12 << 20),
        cost_estimate=pl.CostEstimate(flops=32 * 2 * R**3, bytes_accessed=3 << 20, transcendentals=0),
        name="top_far",
    )(info, src, own, other, mat)


def tail_kernel(info, src, c0, c1, c2, c3, c4a, c4b, c5, c6, c7, mat, down, top, base, both, out, table):
    i = pl.program_id(0)
    x, core, z, y = info[1], info[2], info[3], info[4]

    @pl.when(i == 0)
    def _():
        for s, ref in ((0, c0), (1, c1), (2, c2), (3, c3), (4, c4a), (4.5, c4b), (5, c5), (6, c6), (7, c7)):
            first = int(s * 32)

            def step(j, carry):
                v = ref[pl.ds(pl.multiple_of(j * R, R), R), :]
                table[first + 2 * j] = v[:, :R]
                table[first + 2 * j + 1] = v[:, R:]
                return carry

            lax.fori_loop(0, ref.shape[0] // R, step, 0, unroll=4)

    acc = dot(down[0], top[...])
    rows = []
    for n in range(16):
        g = jnp.clip(src[i, n] - info[5], 0, Z * Y * 8 - 1)
        sy = lax.rem(y - lax.rem(g // 8, Y) + Y, Y)
        sz = lax.rem(z - g // (8 * Y) + Z, Z)
        rows.append(table[(sz * Y + sy) * 8 + lax.rem(g, 8)])
    for q in range(4):
        acc += dot(wide([mat[0, 4 * q + n] for n in range(4)]), jnp.concatenate(rows[4 * q : 4 * q + 4], axis=0))
    local = acc.astype(BF)
    res = dot(both[...].reshape(8 * R, R), local).reshape(8, R, R)
    out[...] = (base[...] + res).astype(BF)


def tail(info, src, chunks, mat, down, top, base, both):
    def const(a):
        return pl.BlockSpec(a.shape, lambda i, *_: (0, 0))

    leaf = pl.BlockSpec((8, R, R), lambda i, *_: (i, 0, 0))
    return pl.pallas_call(
        tail_kernel,
        grid_spec=pltpu.PrefetchScalarGridSpec(
            num_scalar_prefetch=2,
            grid=(8,),
            in_specs=[const(c) for c in chunks]
            + [
                pl.BlockSpec((1, 16, R, R), lambda i, *_: (i, 0, 0, 0)),
                pl.BlockSpec((1, R, R), lambda i, *_: (i, 0, 0)),
                const(top),
                leaf,
                leaf,
            ],
            out_specs=leaf,
            scratch_shapes=[VMEM((256, R, R), BF)],
        ),
        out_shape=jax.ShapeDtypeStruct((64, R, R), BF),
        compiler_params=pltpu.CompilerParams(vmem_limit_bytes=24 << 20),
        cost_estimate=pl.CostEstimate(flops=200 * 2 * R**3, bytes_accessed=9 << 20, transcendentals=0),
        name="tail",
    )(info, src, *chunks, mat, down, top, base, both)


def place(d):
    return d // (CORE * Z * Y), d // (Z * Y) % CORE, d // Y % Z, d % Y


def index(x, c, z, y):
    return ((x % X * CORE + c % CORE) * Z + z % Z) * Y + y % Y


def shift(a, x=0, c=0, z=0, y=0):
    pairs = []
    for d in range(X * CORE * Z * Y):
        px, pc, pz, py = place(d)
        pairs.append((d, index(px + x, pc + c, pz + z, py + y)))
    return lax.ppermute(a, BOTH, pairs)


def halo(a):
    n = X * CORE * Z * Y
    up = [(i, i + 1) for i in range(n - 1)]
    return lax.ppermute(a, BOTH, up), lax.ppermute(a, BOTH, [(j, i) for i, j in up])


def shards(
    charges,
    source_basis,
    target_basis,
    leaf_up,
    mid_up,
    leaf_down,
    mid_down,
    leaf_far_src,
    leaf_far_mat,
    mid_far_src,
    mid_far_mat,
    top_far_src,
    top_far_mat,
    near_src,
    near_count,
    near_mat,
):
    me = lax.axis_index(BOTH).astype(jnp.int32)
    px, pc, pz, py = place(me)
    info = jnp.stack([(me - 1) * 64, px, pc, pz, py, me // (Z * Y) * (Z * Y * 8)])

    packed, coef, mt = upsweep(charges, source_basis, leaf_up, mid_up)

    by_y = [mt] + [shift(mt, y=s) for s in range(1, Y)]
    mids = jnp.concatenate([a[:256] for a in by_y], axis=0)
    tops = jnp.concatenate([a[256:] for a in by_y], axis=0)

    before, after = halo(packed)
    coef_before, coef_after = halo(coef)

    all_z = jnp.concatenate([tops] + [shift(tops, z=s) for s in range(1, Z)], axis=0)
    f1, b1 = shift(mids, z=1), shift(mids, z=-1)
    f2, b2 = shift(f1, z=1), shift(b1, z=-1)
    f3, b3 = shift(f2, z=1), shift(b2, z=-1)
    f4, b4 = shift(f3[:512], z=1), shift(b3[512:], z=-1)

    all_x = jnp.concatenate([all_z] + [shift(all_z, x=s) for s in range(1, X)], axis=0)
    other = shift(all_x, c=1)

    near = near_field(info, near_src.T, near_count, before, packed, after, near_mat)
    base, both = leaf_far(
        info, leaf_far_src.T, coef_before, coef, coef_after, leaf_far_mat, target_basis, leaf_down, near
    )
    top_local = top_far(info, top_far_src, all_x, other, top_far_mat)
    chunks = [mids, f1, f2, f3, f4, b4, b3, b2, b1]
    return tail(info, mid_far_src, chunks, mid_far_mat, mid_down, top_local, base, both)


def solution(mesh):
    row = P(BOTH, None)
    three = P(BOTH, None, None)
    four = P(BOTH, None, None, None)
    in_specs = (
        three, three, three, three, three, three, three,
        row, four, row, four, row, four, row, P(BOTH), four,
    )
    return jax.shard_map(shards, mesh=mesh, in_specs=in_specs, out_specs=three, check_vma=False)
```

```python
import jax
import jax.numpy as jnp
from jax import lax
from jax.experimental import pallas as pl
from jax.experimental.pallas import tpu as pltpu
from jax.sharding import PartitionSpec as P

BOTH = ("cluster", "coupling")
X, CORE, Z, Y = 4, 2, 8, 4
R = 64
BF = jnp.bfloat16
F32 = jnp.float32
VMEM = pltpu.VMEM
BIG = 46 << 20
SMALL = 8 << 20


def dot(a, b):
    return lax.dot_general(a, b, (((1,), (0,)), ((), ())), preferred_element_type=F32)


def dot_t(a, b):
    return lax.dot_general(a, b, (((0,), (0,)), ((), ())), preferred_element_type=F32)


def beside(a, b):
    return jnp.concatenate([a, b], axis=1)


def wide(blocks):
    return jnp.concatenate([beside(a, b) for a, b in zip(blocks[::2], blocks[1::2])], axis=1)


def up_kernel(c_ref, s_ref, lu_ref, mu_ref, pc_ref, pk_ref, mt_ref, acc):
    i = pl.program_id(0)

    @pl.when(i == 0)
    def _():
        acc[...] = jnp.zeros_like(acc)

    coefs = []
    for l in range(16):
        coefs.append(dot_t(s_ref[l], c_ref[l]).astype(BF))
    for j in range(8):
        pc_ref[j] = beside(c_ref[2 * j], c_ref[2 * j + 1])
        pk_ref[j] = beside(coefs[2 * j], coefs[2 * j + 1])
    mids = []
    for h in range(2):
        up = lu_ref[8 * h : 8 * h + 8].reshape(8 * R, R)
        mids.append(dot_t(up, jnp.concatenate(coefs[8 * h : 8 * h + 8], axis=0)).astype(BF))
    mt_ref[pl.ds(pl.multiple_of(i * R, R), R), :] = beside(*mids)
    acc[...] += dot_t(mu_ref[...].reshape(2 * R, R), jnp.concatenate(mids, axis=0))

    @pl.when(i == 3)
    def _():
        top = acc[...].astype(BF)
        mt_ref[256:288, :] = beside(top[:32], top[32:])


def upsweep(charges, source_basis, leaf_up, mid_up):
    leaf = pl.BlockSpec((16, R, R), lambda i: (i, 0, 0))
    pair = pl.BlockSpec((8, R, 2 * R), lambda i: (i, 0, 0))
    return pl.pallas_call(
        up_kernel,
        grid=(4,),
        in_specs=[leaf, leaf, leaf, pl.BlockSpec((2, R, R), lambda i: (i, 0, 0))],
        out_specs=[pair, pair, pl.BlockSpec((288, 128), lambda i: (0, 0))],
        out_shape=[
            jax.ShapeDtypeStruct((32, R, 2 * R), BF),
            jax.ShapeDtypeStruct((32, R, 2 * R), BF),
            jax.ShapeDtypeStruct((288, 128), BF),
        ],
        scratch_shapes=[VMEM((R, R), F32)],
        compiler_params=pltpu.CompilerParams(vmem_limit_bytes=60 << 20),
        cost_estimate=pl.CostEstimate(flops=136 * 2 * R**3, bytes_accessed=5 << 20, transcendentals=0),
        name="upsweep",
    )(charges, source_basis, leaf_up, mid_up)


def copies_of(pairs, sems):
    out = [pltpu.make_async_copy(a, b, sems.at[k]) for k, (a, b) in enumerate(pairs)]
    for c in out:
        c.start()
    return out


def parts(a, b, n):
    w = a.shape[0] // n
    return [(a.at[pl.ds(k * w, w)], b.at[pl.ds(k * w, w)]) for k in range(n)]


def half_masks(mask):
    lane = lax.broadcasted_iota(jnp.int32, (R, 2 * R), 1)
    mask[0] = jnp.where(lane < R, 1.0, 0.0).astype(BF)
    mask[1] = jnp.where(lane < R, 0.0, 1.0).astype(BF)
    mask[2] = jnp.zeros((R, 2 * R), BF)


def fold(acc):
    return acc[:, :R] + acc[:, R:]


def near_kernel(
    info, src, cnt, cb, co, ca, mat, fmat, tb, ld, out, fm, tbv, both, table, mv, ldv, mask, sem
):
    tables = copies_of([(cb, table.at[0:32]), (co, table.at[32:64]), (ca, table.at[64:96])], sem)
    copies_of(parts(mat, mv, 8), sem.at[pl.ds(3, 8)])
    small = copies_of([(tb, tbv), (ld, ldv)], sem.at[pl.ds(11, 2)])
    late = copies_of(parts(fmat, fm, 8), sem.at[pl.ds(13, 8)])
    half_masks(mask)
    for c in tables:
        c.wait()

    def step(c, carry):
        pltpu.make_async_copy(mat.at[pl.ds(8 * c, 8)], mv.at[pl.ds(8 * c, 8)], sem.at[3 + c]).wait()
        for g in range(2):
            accs = []
            for j in range(4):
                l = c * 8 + g * 4 + j
                acc = jnp.zeros((R, 2 * R), F32)
                for n in range(8):
                    k = jnp.clip(src[n, l] - info[0], 0, 191)
                    m = mask[jnp.where(n < cnt[l], k & 1, 2)]
                    acc += dot(mv[l, n], table[k >> 1] * m)
                accs.append(acc)
            for j in range(4):
                out[c * 8 + g * 4 + j] = fold(accs[j])
        return carry

    lax.fori_loop(0, 8, step, 0)
    for c in small:
        c.wait()

    def products(i, carry):
        res = [dot(tbv[8 * i + j], ldv[8 * i + j]).astype(BF) for j in range(8)]
        for j in range(8):
            both[8 * i + j] = res[j]
        return carry

    lax.fori_loop(0, 8, products, 0)
    for c in late:
        c.wait()


def near_field(info, src, cnt, charges, mat, fmat, tb, ld):
    v = pl.BlockSpec(memory_space=VMEM)
    s = pl.BlockSpec(memory_space=pltpu.SMEM)
    mats, leaf = VMEM((64, 8, R, R), BF), VMEM((64, R, R), BF)
    return pl.pallas_call(
        near_kernel,
        in_specs=[s] * 3 + [pl.BlockSpec(memory_space=pl.ANY)] * 7,
        out_specs=[v] * 4,
        out_shape=[VMEM((64, R, R), F32), mats, leaf, leaf],
        scratch_shapes=[
            VMEM((96, R, 2 * R), BF),
            mats,
            leaf,
            VMEM((3, R, 2 * R), BF),
            pltpu.SemaphoreType.DMA((21,)),
        ],
        compiler_params=pltpu.CompilerParams(vmem_limit_bytes=BIG),
        cost_estimate=pl.CostEstimate(flops=576 * 2 * R**3, bytes_accessed=24 << 20, transcendentals=0),
        name="near",
    )(info, src, cnt, *charges, mat, fmat, tb, ld)


def far_kernel(info, src, ku, ko, kd, mv, tbv, near, base, table, far, mask, sem):
    tables = copies_of([(ku, table.at[0:32]), (ko, table.at[32:64]), (kd, table.at[64:96])], sem)
    half_masks(mask)
    for c in tables:
        c.wait()

    def leaf(c, carry):
        for g in range(2):
            accs = []
            for j in range(4):
                l = c * 8 + g * 4 + j
                acc = jnp.zeros((R, 2 * R), F32)
                for n in range(8):
                    k = jnp.clip(src[n, l] - info[0], 0, 191)
                    acc += dot(mv[l, n], table[k >> 1] * mask[k & 1])
                accs.append(acc)
            for j in range(4):
                far[c * 8 + g * 4 + j] = fold(accs[j]).astype(BF)
        return carry

    lax.fori_loop(0, 8, leaf, 0)

    def last(i, carry):
        res = [near[8 * i + j] + dot(tbv[8 * i + j], far[8 * i + j]) for j in range(8)]
        for j in range(8):
            base[8 * i + j] = res[j]
        return carry

    lax.fori_loop(0, 8, last, 0)


def leaf_far(info, src, coefs, mat, tb, near):
    v = pl.BlockSpec(memory_space=VMEM)
    s = pl.BlockSpec(memory_space=pltpu.SMEM)
    return pl.pallas_call(
        far_kernel,
        in_specs=[s] * 2 + [pl.BlockSpec(memory_space=pl.ANY)] * 3 + [v] * 3,
        out_specs=v,
        out_shape=VMEM((64, R, R), F32),
        scratch_shapes=[
            VMEM((96, R, 2 * R), BF),
            VMEM((64, R, R), BF),
            VMEM((3, R, 2 * R), BF),
            pltpu.SemaphoreType.DMA((3,)),
        ],
        compiler_params=pltpu.CompilerParams(vmem_limit_bytes=32 << 20),
        cost_estimate=pl.CostEstimate(flops=576 * 2 * R**3, bytes_accessed=16 << 20, transcendentals=0),
        name="leaf_far",
    )(info, src, *coefs, mat, tb, near)


def pick_kernel(*refs):
    rings, out, sem = refs[:16], refs[16], refs[17]
    pairs = []
    for s in range(8):
        for h in range(2):
            for k in range(2):
                q = 4 * s + 2 * h + k
                pairs.append((rings[2 * s + h].at[pl.ds(288 * k + 256, 32)], out.at[pl.ds(32 * q, 32)]))
    for c in copies_of(pairs, sem):
        c.wait()


def pick_tops(rings):
    return pl.pallas_call(
        pick_kernel,
        in_specs=[pl.BlockSpec(memory_space=pl.ANY)] * 16,
        out_specs=pl.BlockSpec(memory_space=VMEM),
        out_shape=VMEM((1024, 128), BF),
        scratch_shapes=[pltpu.SemaphoreType.DMA((32,))],
        compiler_params=pltpu.CompilerParams(vmem_limit_bytes=SMALL),
        cost_estimate=pl.CostEstimate(flops=0, bytes_accessed=1 << 20, transcendentals=0),
        name="pick_tops",
    )(*rings)


def join_kernel(a, b, c, d, out, sem):
    n = a.shape[0]
    for copy in copies_of([(r, out.at[pl.ds(k * n, n)]) for k, r in enumerate((a, b, c, d))], sem):
        copy.wait()


def join(arrays):
    return pl.pallas_call(
        join_kernel,
        in_specs=[pl.BlockSpec(memory_space=pl.ANY)] * 4,
        out_specs=pl.BlockSpec(memory_space=VMEM),
        out_shape=VMEM((4096, 128), BF),
        scratch_shapes=[pltpu.SemaphoreType.DMA((4,))],
        compiler_params=pltpu.CompilerParams(vmem_limit_bytes=SMALL),
        cost_estimate=pl.CostEstimate(flops=0, bytes_accessed=2 << 20, transcendentals=0),
        name="join",
    )(*arrays)


def top_kernel(info, src, own, other, mat, out):
    x, core, z, y = info[1], info[2], info[3], info[4]
    acc = jnp.zeros((R, R), F32)
    rows = []
    for n in range(32):
        g = jnp.clip(src[0, n], 0, X * CORE * Z * Y - 1)
        sy = (y - g) & 3
        sz = (z - (g >> 2)) & 7
        sx = (x - (g >> 6)) & 3
        same = ((g >> 5) & 1) == core
        at = pl.ds(pl.multiple_of(((sx * Z + sz) * Y + sy) * 32, 32), 32)
        t = jnp.where(same, own[at, :], other[at, :])
        rows += [t[:, :R], t[:, R:]]
    for q in range(8):
        acc += dot(wide([mat[0, 4 * q + n] for n in range(4)]), jnp.concatenate(rows[8 * q : 8 * q + 8], axis=0))
    out[...] = acc.astype(BF)


def top_far(info, src, own, other, mat):
    v = pl.BlockSpec(memory_space=VMEM)
    s = pl.BlockSpec(memory_space=pltpu.SMEM)
    return pl.pallas_call(
        top_kernel,
        in_specs=[s, s, v, v, v],
        out_specs=v,
        out_shape=jax.ShapeDtypeStruct((R, R), BF),
        compiler_params=pltpu.CompilerParams(vmem_limit_bytes=SMALL),
        cost_estimate=pl.CostEstimate(flops=32 * 2 * R**3, bytes_accessed=3 << 20, transcendentals=0),
        name="top_far",
    )(info, src, own, other, mat)


def mid_kernel(info, src, mat, *refs):
    rings, (out, raw, mv, mask, sem) = refs[:16], refs[16:]
    z, y = info[3], info[4]
    copies = copies_of([(rings[s], raw.at[s]) for s in range(16)], sem)
    copies += copies_of(parts(mat, mv, 8), sem.at[pl.ds(16, 8)])
    half_masks(mask)
    for c in copies:
        c.wait()
    done = []
    for p in range(8):
        acc = jnp.zeros((R, 2 * R), F32)
        for n in range(16):
            g = jnp.clip(src[p, n] - info[5], 0, Z * Y * 8 - 1)
            sy = (y - (g >> 3)) & 3
            sz = (z - (g >> 5)) & 7
            at = (sy & 1) * 288 + ((g >> 1) & 3) * R
            t = raw[sz * 2 + (sy >> 1), pl.ds(pl.multiple_of(at, 32), R), :]
            acc += dot(mv[p, n], t * mask[g & 1])
        done.append(fold(acc))
    for p in range(8):
        out[p] = done[p]


def mid_far(info, src, mat, rings):
    v = pl.BlockSpec(memory_space=VMEM)
    s = pl.BlockSpec(memory_space=pltpu.SMEM)
    return pl.pallas_call(
        mid_kernel,
        in_specs=[s, s] + [pl.BlockSpec(memory_space=pl.ANY)] * 17,
        out_specs=v,
        out_shape=VMEM((8, R, R), F32),
        scratch_shapes=[
            VMEM((16, 576, 128), BF), VMEM(mat.shape, BF), VMEM((3, R, 2 * R), BF), pltpu.SemaphoreType.DMA((24,)),
        ],
        compiler_params=pltpu.CompilerParams(vmem_limit_bytes=12 << 20),
        cost_estimate=pl.CostEstimate(flops=128 * 2 * R**3, bytes_accessed=6 << 20, transcendentals=0),
        name="mid_far",
    )(info, src, mat, *rings)


def tail_kernel(top_ref, far, down, base, both, out, buf, sem):
    top = top_ref[...]
    local = [(far[p] + dot(down[p], top)).astype(BF) for p in range(8)]
    copies = []
    for p in range(8):
        at = pl.ds(8 * p, 8)
        res = dot(both[at].reshape(8 * R, R), local[p]).reshape(8, R, R)
        buf[at] = (base[at] + res).astype(BF)
        copies.append(pltpu.make_async_copy(buf.at[at], out.at[at], sem.at[p]))
        copies[-1].start()
    for c in copies:
        c.wait()


def tail(top, far, down, base, both):
    v = pl.BlockSpec(memory_space=VMEM)
    return pl.pallas_call(
        tail_kernel,
        in_specs=[v] * 5,
        out_specs=pl.BlockSpec(memory_space=pltpu.HBM),
        out_shape=jax.ShapeDtypeStruct((64, R, R), BF),
        scratch_shapes=[VMEM((64, R, R), BF), pltpu.SemaphoreType.DMA((8,))],
        compiler_params=pltpu.CompilerParams(vmem_limit_bytes=SMALL),
        cost_estimate=pl.CostEstimate(flops=72 * 2 * R**3, bytes_accessed=6 << 20, transcendentals=0),
        name="tail",
    )(top, far, down, base, both)


def place(d):
    return d // (CORE * Z * Y), d // (Z * Y) % CORE, d // Y % Z, d % Y


def index(x, c, z, y):
    return ((x % X * CORE + c % CORE) * Z + z % Z) * Y + y % Y


def shift(a, x=0, c=0, z=0, y=0):
    pairs = []
    for d in range(X * CORE * Z * Y):
        px, pc, pz, py = place(d)
        pairs.append((d, index(px + x, pc + c, pz + z, py + y)))
    return lax.ppermute(a, BOTH, pairs)


def some(a, pairs):
    return lax.ppermute(a, BOTH, pairs)


def halo(a):
    n = X * CORE * Z * Y
    up = [(i, i + 1) for i in range(n - 1)]
    return some(a, up), some(a, [(j, i) for i, j in up])


def tie(*arrays):
    return lax.optimization_barrier(arrays)


def shards(
    charges,
    source_basis,
    target_basis,
    leaf_up,
    mid_up,
    leaf_down,
    mid_down,
    leaf_far_src,
    leaf_far_mat,
    mid_far_src,
    mid_far_mat,
    top_far_src,
    top_far_mat,
    near_src,
    near_count,
    near_mat,
):
    me = lax.axis_index(BOTH).astype(jnp.int32)
    px, pc, pz, py = place(me)
    info = jnp.stack([(me - 1) * 64, px, pc, pz, py, me // (Z * Y) * (Z * Y * 8)])

    packed, coef, mt = upsweep(charges, source_basis, leaf_up, mid_up)

    m1, m3, m2 = shift(mt, y=1), shift(mt, y=-1), shift(mt, y=2)
    rings = {(0, 0): jnp.concatenate([mt, m1], axis=0), (0, 1): jnp.concatenate([m2, m3], axis=0)}
    for s in range(1, 4):
        for h in range(2):
            rings[s, h] = shift(rings[s - 1, h], z=1)
            rings[8 - s, h] = shift(rings[(9 - s) % 8, h], z=-1)
    rings[4, 0] = shift(rings[3, 0], z=1)
    rings[4, 1] = shift(rings[5, 1], z=-1)
    rings = [rings[s, h] for s in range(8) for h in range(2)]

    all_z = pick_tops(rings)
    all_z, rings[0], packed = tie(all_z, rings[0], packed)
    by_x = [all_z] + [shift(all_z, x=s) for s in range(1, X)]
    before, after = halo(packed)
    far = mid_far(info, mid_far_src, mid_far_mat, rings)
    *by_x, coef, packed, far = tie(*by_x, coef, packed, far)
    all_x = join(by_x)
    other = shift(all_x, c=1)
    coef_before, coef_after = halo(coef)
    near, far_v, tb_v, both = near_field(
        info, near_src.T, near_count, (before, packed, after), near_mat, leaf_far_mat, target_basis, leaf_down
    )
    base = leaf_far(info, leaf_far_src.T, (coef_before, coef, coef_after), far_v, tb_v, near)
    top_local = top_far(info, top_far_src, all_x, other, top_far_mat)
    return tail(top_local, far, mid_down, base, both)


def solution(mesh):
    row = P(BOTH, None)
    three = P(BOTH, None, None)
    four = P(BOTH, None, None, None)
    in_specs = (
        three, three, three, three, three, three, three,
        row, four, row, four, row, four, row, P(BOTH), four,
    )
    return jax.shard_map(shards, mesh=mesh, in_specs=in_specs, out_specs=three, check_vma=False)
```

```python
import jax
import jax.numpy as jnp
from jax import lax
from jax.experimental import pallas as pl
from jax.experimental.pallas import tpu as pltpu
from jax.sharding import PartitionSpec as P

BOTH = ("cluster", "coupling")
X, CORE, Z, Y = 4, 2, 8, 4
R = 64
BF = jnp.bfloat16
F32 = jnp.float32
VMEM = pltpu.VMEM
BIG = 46 << 20
SMALL = 8 << 20


def dot(a, b):
    return lax.dot_general(a, b, (((1,), (0,)), ((), ())), preferred_element_type=F32)


def dot_t(a, b):
    return lax.dot_general(a, b, (((0,), (0,)), ((), ())), preferred_element_type=F32)


def beside(a, b):
    return jnp.concatenate([a, b], axis=1)


def wide(blocks):
    return jnp.concatenate([beside(a, b) for a, b in zip(blocks[::2], blocks[1::2])], axis=1)


def up_kernel(c_ref, s_ref, lu_ref, mu_ref, pc_ref, pk_ref, mt_ref, acc):
    i = pl.program_id(0)

    @pl.when(i == 0)
    def _():
        acc[...] = jnp.zeros_like(acc)

    coefs = []
    for l in range(16):
        coefs.append(dot_t(s_ref[l], c_ref[l]).astype(BF))
    for j in range(8):
        pc_ref[j] = beside(c_ref[2 * j], c_ref[2 * j + 1])
        pk_ref[j] = beside(coefs[2 * j], coefs[2 * j + 1])
    mids = []
    for h in range(2):
        up = lu_ref[8 * h : 8 * h + 8].reshape(8 * R, R)
        mids.append(dot_t(up, jnp.concatenate(coefs[8 * h : 8 * h + 8], axis=0)).astype(BF))
    mt_ref[pl.ds(pl.multiple_of(i * R, R), R), :] = beside(*mids)
    acc[...] += dot_t(mu_ref[...].reshape(2 * R, R), jnp.concatenate(mids, axis=0))

    @pl.when(i == 3)
    def _():
        top = acc[...].astype(BF)
        mt_ref[256:288, :] = beside(top[:32], top[32:])


def upsweep(charges, source_basis, leaf_up, mid_up):
    leaf = pl.BlockSpec((16, R, R), lambda i: (i, 0, 0))
    pair = pl.BlockSpec((8, R, 2 * R), lambda i: (i, 0, 0))
    return pl.pallas_call(
        up_kernel,
        grid=(4,),
        in_specs=[leaf, leaf, leaf, pl.BlockSpec((2, R, R), lambda i: (i, 0, 0))],
        out_specs=[pair, pair, pl.BlockSpec((288, 128), lambda i: (0, 0))],
        out_shape=[
            jax.ShapeDtypeStruct((32, R, 2 * R), BF),
            jax.ShapeDtypeStruct((32, R, 2 * R), BF),
            jax.ShapeDtypeStruct((288, 128), BF),
        ],
        scratch_shapes=[VMEM((R, R), F32)],
        compiler_params=pltpu.CompilerParams(vmem_limit_bytes=60 << 20),
        cost_estimate=pl.CostEstimate(flops=136 * 2 * R**3, bytes_accessed=5 << 20, transcendentals=0),
        name="upsweep",
    )(charges, source_basis, leaf_up, mid_up)


def copies_of(pairs, sems):
    out = [pltpu.make_async_copy(a, b, sems.at[k]) for k, (a, b) in enumerate(pairs)]
    for c in out:
        c.start()
    return out


def parts(a, b, n):
    w = a.shape[0] // n
    return [(a.at[pl.ds(k * w, w)], b.at[pl.ds(k * w, w)]) for k in range(n)]


def half_masks(mask):
    lane = lax.broadcasted_iota(jnp.int32, (R, 2 * R), 1)
    mask[0] = jnp.where(lane < R, 1.0, 0.0).astype(BF)
    mask[1] = jnp.where(lane < R, 0.0, 1.0).astype(BF)
    mask[2] = jnp.zeros((R, 2 * R), BF)


def fold(acc):
    return acc[:, :R] + acc[:, R:]


def near_kernel(
    info, src, cnt, cb, co, ca, mat, fmat, tb, ld, out, fm, tbv, both, table, mv, ldv, mask, sem
):
    tables = copies_of([(cb, table.at[0:32]), (co, table.at[32:64]), (ca, table.at[64:96])], sem)
    copies_of(parts(mat, mv, 8), sem.at[pl.ds(3, 8)])
    small = copies_of([(tb, tbv), (ld, ldv)], sem.at[pl.ds(11, 2)])
    late = copies_of(parts(fmat, fm, 8), sem.at[pl.ds(13, 8)])
    half_masks(mask)
    for c in tables:
        c.wait()

    def step(c, carry):
        pltpu.make_async_copy(mat.at[pl.ds(8 * c, 8)], mv.at[pl.ds(8 * c, 8)], sem.at[3 + c]).wait()
        for g in range(2):
            accs = []
            for j in range(4):
                l = c * 8 + g * 4 + j
                acc = jnp.zeros((R, 2 * R), F32)
                for n in range(8):
                    k = jnp.clip(src[n, l] - info[0], 0, 191)
                    m = mask[jnp.where(n < cnt[l], k & 1, 2)]
                    acc += dot(mv[l, n], table[k >> 1] * m)
                accs.append(acc)
            for j in range(4):
                out[c * 8 + g * 4 + j] = fold(accs[j])
        return carry

    lax.fori_loop(0, 8, step, 0)
    for c in small:
        c.wait()

    def products(i, carry):
        res = [dot(tbv[8 * i + j], ldv[8 * i + j]).astype(BF) for j in range(8)]
        for j in range(8):
            both[8 * i + j] = res[j]
        return carry

    lax.fori_loop(0, 8, products, 0)
    for c in late:
        c.wait()


def near_field(info, src, cnt, charges, mat, fmat, tb, ld):
    v = pl.BlockSpec(memory_space=VMEM)
    s = pl.BlockSpec(memory_space=pltpu.SMEM)
    mats, leaf = VMEM((64, 8, R, R), BF), VMEM((64, R, R), BF)
    return pl.pallas_call(
        near_kernel,
        in_specs=[s] * 3 + [pl.BlockSpec(memory_space=pl.ANY)] * 7,
        out_specs=[v] * 4,
        out_shape=[VMEM((64, R, R), F32), mats, leaf, leaf],
        scratch_shapes=[
            VMEM((96, R, 2 * R), BF),
            mats,
            leaf,
            VMEM((3, R, 2 * R), BF),
            pltpu.SemaphoreType.DMA((21,)),
        ],
        compiler_params=pltpu.CompilerParams(vmem_limit_bytes=BIG),
        cost_estimate=pl.CostEstimate(flops=576 * 2 * R**3, bytes_accessed=24 << 20, transcendentals=0),
        name="near",
    )(info, src, cnt, *charges, mat, fmat, tb, ld)


def far_kernel(info, src, ku, ko, kd, mv, tbv, near, base, table, far, mask, sem):
    tables = copies_of([(ku, table.at[0:32]), (ko, table.at[32:64]), (kd, table.at[64:96])], sem)
    half_masks(mask)
    for c in tables:
        c.wait()

    def leaf(c, carry):
        for g in range(2):
            accs = []
            for j in range(4):
                l = c * 8 + g * 4 + j
                acc = jnp.zeros((R, 2 * R), F32)
                for n in range(8):
                    k = jnp.clip(src[n, l] - info[0], 0, 191)
                    acc += dot(mv[l, n], table[k >> 1] * mask[k & 1])
                accs.append(acc)
            for j in range(4):
                far[c * 8 + g * 4 + j] = fold(accs[j]).astype(BF)
        return carry

    lax.fori_loop(0, 8, leaf, 0)

    def last(i, carry):
        res = [near[8 * i + j] + dot(tbv[8 * i + j], far[8 * i + j]) for j in range(8)]
        for j in range(8):
            base[8 * i + j] = res[j]
        return carry

    lax.fori_loop(0, 8, last, 0)


def leaf_far(info, src, coefs, mat, tb, near):
    v = pl.BlockSpec(memory_space=VMEM)
    s = pl.BlockSpec(memory_space=pltpu.SMEM)
    return pl.pallas_call(
        far_kernel,
        in_specs=[s] * 2 + [pl.BlockSpec(memory_space=pl.ANY)] * 3 + [v] * 3,
        out_specs=v,
        out_shape=VMEM((64, R, R), F32),
        scratch_shapes=[
            VMEM((96, R, 2 * R), BF),
            VMEM((64, R, R), BF),
            VMEM((3, R, 2 * R), BF),
            pltpu.SemaphoreType.DMA((3,)),
        ],
        compiler_params=pltpu.CompilerParams(vmem_limit_bytes=32 << 20),
        cost_estimate=pl.CostEstimate(flops=576 * 2 * R**3, bytes_accessed=16 << 20, transcendentals=0),
        name="leaf_far",
    )(info, src, *coefs, mat, tb, near)


def pick_kernel(*refs):
    rings, out, sem = refs[:16], refs[16], refs[17]
    pairs = []
    for s in range(8):
        for h in range(2):
            for k in range(2):
                q = 4 * s + 2 * h + k
                pairs.append((rings[2 * s + h].at[pl.ds(288 * k + 256, 32)], out.at[pl.ds(32 * q, 32)]))
    for c in copies_of(pairs, sem):
        c.wait()


def pick_tops(rings):
    return pl.pallas_call(
        pick_kernel,
        in_specs=[pl.BlockSpec(memory_space=pl.ANY)] * 16,
        out_specs=pl.BlockSpec(memory_space=VMEM),
        out_shape=VMEM((1024, 128), BF),
        scratch_shapes=[pltpu.SemaphoreType.DMA((32,))],
        compiler_params=pltpu.CompilerParams(vmem_limit_bytes=SMALL),
        cost_estimate=pl.CostEstimate(flops=0, bytes_accessed=1 << 20, transcendentals=0),
        name="pick_tops",
    )(*rings)


def join_kernel(a, b, c, d, out, sem):
    n = a.shape[0]
    for copy in copies_of([(r, out.at[pl.ds(k * n, n)]) for k, r in enumerate((a, b, c, d))], sem):
        copy.wait()


def join(arrays):
    return pl.pallas_call(
        join_kernel,
        in_specs=[pl.BlockSpec(memory_space=pl.ANY)] * 4,
        out_specs=pl.BlockSpec(memory_space=VMEM),
        out_shape=VMEM((4096, 128), BF),
        scratch_shapes=[pltpu.SemaphoreType.DMA((4,))],
        compiler_params=pltpu.CompilerParams(vmem_limit_bytes=SMALL),
        cost_estimate=pl.CostEstimate(flops=0, bytes_accessed=2 << 20, transcendentals=0),
        name="join",
    )(*arrays)


def top_kernel(info, src, own, other, mat, out):
    x, core, z, y = info[1], info[2], info[3], info[4]
    acc = jnp.zeros((R, R), F32)
    rows = []
    for n in range(32):
        g = jnp.clip(src[0, n], 0, X * CORE * Z * Y - 1)
        sy = (y - g) & 3
        sz = (z - (g >> 2)) & 7
        sx = (x - (g >> 6)) & 3
        same = ((g >> 5) & 1) == core
        at = pl.ds(pl.multiple_of(((sx * Z + sz) * Y + sy) * 32, 32), 32)
        t = jnp.where(same, own[at, :], other[at, :])
        rows += [t[:, :R], t[:, R:]]
    for q in range(8):
        acc += dot(wide([mat[0, 4 * q + n] for n in range(4)]), jnp.concatenate(rows[8 * q : 8 * q + 8], axis=0))
    out[...] = acc.astype(BF)


def top_far(info, src, own, other, mat):
    v = pl.BlockSpec(memory_space=VMEM)
    s = pl.BlockSpec(memory_space=pltpu.SMEM)
    return pl.pallas_call(
        top_kernel,
        in_specs=[s, s, v, v, v],
        out_specs=v,
        out_shape=jax.ShapeDtypeStruct((R, R), BF),
        compiler_params=pltpu.CompilerParams(vmem_limit_bytes=SMALL),
        cost_estimate=pl.CostEstimate(flops=32 * 2 * R**3, bytes_accessed=3 << 20, transcendentals=0),
        name="top_far",
    )(info, src, own, other, mat)


def mid_kernel(info, src, mat, *refs):
    rings, (out, raw, mv, mask, sem) = refs[:16], refs[16:]
    z, y = info[3], info[4]
    copies = copies_of([(rings[s], raw.at[s]) for s in range(16)], sem)
    copies += copies_of(parts(mat, mv, 8), sem.at[pl.ds(16, 8)])
    half_masks(mask)
    for c in copies:
        c.wait()
    done = []
    for p in range(8):
        acc = jnp.zeros((R, 2 * R), F32)
        for n in range(16):
            g = jnp.clip(src[p, n] - info[5], 0, Z * Y * 8 - 1)
            sy = (y - (g >> 3)) & 3
            sz = (z - (g >> 5)) & 7
            at = (sy & 1) * 288 + ((g >> 1) & 3) * R
            t = raw[sz * 2 + (sy >> 1), pl.ds(pl.multiple_of(at, 32), R), :]
            acc += dot(mv[p, n], t * mask[g & 1])
        done.append(fold(acc))
    for p in range(8):
        out[p] = done[p]


def mid_far(info, src, mat, rings):
    v = pl.BlockSpec(memory_space=VMEM)
    s = pl.BlockSpec(memory_space=pltpu.SMEM)
    return pl.pallas_call(
        mid_kernel,
        in_specs=[s, s] + [pl.BlockSpec(memory_space=pl.ANY)] * 17,
        out_specs=v,
        out_shape=VMEM((8, R, R), F32),
        scratch_shapes=[
            VMEM((16, 576, 128), BF), VMEM(mat.shape, BF), VMEM((3, R, 2 * R), BF), pltpu.SemaphoreType.DMA((24,)),
        ],
        compiler_params=pltpu.CompilerParams(vmem_limit_bytes=12 << 20),
        cost_estimate=pl.CostEstimate(flops=128 * 2 * R**3, bytes_accessed=6 << 20, transcendentals=0),
        name="mid_far",
    )(info, src, mat, *rings)


def tail_kernel(top_ref, far, down, base, both, out, buf, sem):
    top = top_ref[...]
    local = [(far[p] + dot(down[p], top)).astype(BF) for p in range(8)]
    copies = []
    for p in range(8):
        at = pl.ds(8 * p, 8)
        res = dot(both[at].reshape(8 * R, R), local[p]).reshape(8, R, R)
        buf[at] = (base[at] + res).astype(BF)
        copies.append(pltpu.make_async_copy(buf.at[at], out.at[at], sem.at[p]))
        copies[-1].start()
    for c in copies:
        c.wait()


def tail(top, far, down, base, both):
    v = pl.BlockSpec(memory_space=VMEM)
    return pl.pallas_call(
        tail_kernel,
        in_specs=[v] * 5,
        out_specs=pl.BlockSpec(memory_space=pltpu.HBM),
        out_shape=jax.ShapeDtypeStruct((64, R, R), BF),
        scratch_shapes=[VMEM((64, R, R), BF), pltpu.SemaphoreType.DMA((8,))],
        compiler_params=pltpu.CompilerParams(vmem_limit_bytes=SMALL),
        cost_estimate=pl.CostEstimate(flops=72 * 2 * R**3, bytes_accessed=6 << 20, transcendentals=0),
        name="tail",
    )(top, far, down, base, both)


def place(d):
    return d // (CORE * Z * Y), d // (Z * Y) % CORE, d // Y % Z, d % Y


def index(x, c, z, y):
    return ((x % X * CORE + c % CORE) * Z + z % Z) * Y + y % Y


def shift(a, x=0, c=0, z=0, y=0):
    pairs = []
    for d in range(X * CORE * Z * Y):
        px, pc, pz, py = place(d)
        pairs.append((d, index(px + x, pc + c, pz + z, py + y)))
    return lax.ppermute(a, BOTH, pairs)


def some(a, pairs):
    return lax.ppermute(a, BOTH, pairs)


def halo(a):
    n = X * CORE * Z * Y
    up = [(i, i + 1) for i in range(n - 1)]
    return some(a, up), some(a, [(j, i) for i, j in up])


def tie(*arrays):
    return lax.optimization_barrier(arrays)


def shards(
    charges,
    source_basis,
    target_basis,
    leaf_up,
    mid_up,
    leaf_down,
    mid_down,
    leaf_far_src,
    leaf_far_mat,
    mid_far_src,
    mid_far_mat,
    top_far_src,
    top_far_mat,
    near_src,
    near_count,
    near_mat,
):
    me = lax.axis_index(BOTH).astype(jnp.int32)
    px, pc, pz, py = place(me)
    info = jnp.stack([(me - 1) * 64, px, pc, pz, py, me // (Z * Y) * (Z * Y * 8)])

    packed, coef, mt = upsweep(charges, source_basis, leaf_up, mid_up)

    m1, m3, m2 = shift(mt, y=1), shift(mt, y=-1), shift(mt, y=2)
    rings = {(0, 0): jnp.concatenate([mt, m1], axis=0), (0, 1): jnp.concatenate([m2, m3], axis=0)}
    for s in range(1, 4):
        for h in range(2):
            rings[s, h] = shift(rings[s - 1, h], z=1)
            rings[8 - s, h] = shift(rings[(9 - s) % 8, h], z=-1)
    rings[4, 0] = shift(rings[3, 0], z=1)
    rings[4, 1] = shift(rings[5, 1], z=-1)
    rings = [rings[s, h] for s in range(8) for h in range(2)]

    all_z = pick_tops(rings)
    all_z, rings[0], packed = tie(all_z, rings[0], packed)
    by_x = [all_z] + [shift(all_z, x=s) for s in range(1, X)]
    before, after = halo(packed)
    far = mid_far(info, mid_far_src, mid_far_mat, rings)
    coef, packed, far = tie(coef, packed, far)
    coef_before, coef_after = halo(coef)
    near, far_v, tb_v, both = near_field(
        info, near_src.T, near_count, (before, packed, after), near_mat, leaf_far_mat, target_basis, leaf_down
    )
    by_x[1], near, coef_before, coef_after = tie(by_x[1], near, coef_before, coef_after)
    all_x = join(by_x)
    other = shift(all_x, c=1)
    base = leaf_far(info, leaf_far_src.T, (coef_before, coef, coef_after), far_v, tb_v, near)
    top_local = top_far(info, top_far_src, all_x, other, top_far_mat)
    return tail(top_local, far, mid_down, base, both)


def solution(mesh):
    row = P(BOTH, None)
    three = P(BOTH, None, None)
    four = P(BOTH, None, None, None)
    in_specs = (
        three, three, three, three, three, three, three,
        row, four, row, four, row, four, row, P(BOTH), four,
    )
    return jax.shard_map(shards, mesh=mesh, in_specs=in_specs, out_specs=three, check_vma=False)
```

```python
import jax
import jax.numpy as jnp
from jax import lax
from jax.experimental import pallas as pl
from jax.experimental.pallas import tpu as pltpu
from jax.sharding import PartitionSpec as P

BOTH = ("cluster", "coupling")
X, CORE, Z, Y = 4, 2, 8, 4
R = 64
BF = jnp.bfloat16
F32 = jnp.float32
VMEM = pltpu.VMEM
BIG = 46 << 20
SMALL = 8 << 20


def dot(a, b):
    return lax.dot_general(a, b, (((1,), (0,)), ((), ())), preferred_element_type=F32)


def dot_t(a, b):
    return lax.dot_general(a, b, (((0,), (0,)), ((), ())), preferred_element_type=F32)


def beside(a, b):
    return jnp.concatenate([a, b], axis=1)


def wide(blocks):
    return jnp.concatenate([beside(a, b) for a, b in zip(blocks[::2], blocks[1::2])], axis=1)


def up_kernel(c_ref, s_ref, lu_ref, mu_ref, pc_ref, pk_ref, mt_ref, acc):
    i = pl.program_id(0)

    @pl.when(i == 0)
    def _():
        acc[...] = jnp.zeros_like(acc)

    coefs = []
    for l in range(16):
        coefs.append(dot_t(s_ref[l], c_ref[l]).astype(BF))
    for j in range(8):
        pc_ref[j] = beside(c_ref[2 * j], c_ref[2 * j + 1])
        pk_ref[j] = beside(coefs[2 * j], coefs[2 * j + 1])
    mids = []
    for h in range(2):
        up = lu_ref[8 * h : 8 * h + 8].reshape(8 * R, R)
        mids.append(dot_t(up, jnp.concatenate(coefs[8 * h : 8 * h + 8], axis=0)).astype(BF))
    mt_ref[pl.ds(pl.multiple_of(i * R, R), R), :] = beside(*mids)
    acc[...] += dot_t(mu_ref[...].reshape(2 * R, R), jnp.concatenate(mids, axis=0))

    @pl.when(i == 3)
    def _():
        top = acc[...].astype(BF)
        mt_ref[256:288, :] = beside(top[:32], top[32:])


def upsweep(charges, source_basis, leaf_up, mid_up):
    leaf = pl.BlockSpec((16, R, R), lambda i: (i, 0, 0))
    pair = pl.BlockSpec((8, R, 2 * R), lambda i: (i, 0, 0))
    return pl.pallas_call(
        up_kernel,
        grid=(4,),
        in_specs=[leaf, leaf, leaf, pl.BlockSpec((2, R, R), lambda i: (i, 0, 0))],
        out_specs=[pair, pair, pl.BlockSpec((288, 128), lambda i: (0, 0))],
        out_shape=[
            jax.ShapeDtypeStruct((32, R, 2 * R), BF),
            jax.ShapeDtypeStruct((32, R, 2 * R), BF),
            jax.ShapeDtypeStruct((288, 128), BF),
        ],
        scratch_shapes=[VMEM((R, R), F32)],
        compiler_params=pltpu.CompilerParams(vmem_limit_bytes=60 << 20),
        cost_estimate=pl.CostEstimate(flops=136 * 2 * R**3, bytes_accessed=5 << 20, transcendentals=0),
        name="upsweep",
    )(charges, source_basis, leaf_up, mid_up)


def copies_of(pairs, sems):
    out = [pltpu.make_async_copy(a, b, sems.at[k]) for k, (a, b) in enumerate(pairs)]
    for c in out:
        c.start()
    return out


def parts(a, b, n):
    w = a.shape[0] // n
    return [(a.at[pl.ds(k * w, w)], b.at[pl.ds(k * w, w)]) for k in range(n)]


def half_masks(mask):
    lane = lax.broadcasted_iota(jnp.int32, (R, 2 * R), 1)
    mask[0] = jnp.where(lane < R, 1.0, 0.0).astype(BF)
    mask[1] = jnp.where(lane < R, 0.0, 1.0).astype(BF)
    mask[2] = jnp.zeros((R, 2 * R), BF)


def fold(acc):
    return acc[:, :R] + acc[:, R:]


def near_kernel(
    info, src, cnt, cb, co, ca, mat, fmat, tb, ld, out, fm, tbv, both, table, mv, ldv, mask, sem
):
    tables = copies_of([(cb, table.at[0:32]), (co, table.at[32:64]), (ca, table.at[64:96])], sem)
    copies_of(parts(mat, mv, 8), sem.at[pl.ds(3, 8)])
    small = copies_of([(tb, tbv), (ld, ldv)], sem.at[pl.ds(11, 2)])
    late = copies_of(parts(fmat, fm, 8), sem.at[pl.ds(13, 8)])
    half_masks(mask)
    for c in tables:
        c.wait()

    def step(c, carry):
        pltpu.make_async_copy(mat.at[pl.ds(8 * c, 8)], mv.at[pl.ds(8 * c, 8)], sem.at[3 + c]).wait()
        for g in range(2):
            accs = []
            for j in range(4):
                l = c * 8 + g * 4 + j
                acc = jnp.zeros((R, 2 * R), F32)
                for n in range(8):
                    k = jnp.clip(src[n, l] - info[0], 0, 191)
                    m = mask[jnp.where(n < cnt[l], k & 1, 2)]
                    acc += dot(mv[l, n], table[k >> 1] * m)
                accs.append(acc)
            for j in range(4):
                out[c * 8 + g * 4 + j] = fold(accs[j])
        return carry

    lax.fori_loop(0, 8, step, 0)
    for c in small:
        c.wait()

    def products(i, carry):
        res = [dot(tbv[8 * i + j], ldv[8 * i + j]).astype(BF) for j in range(8)]
        for j in range(8):
            both[8 * i + j] = res[j]
        return carry

    lax.fori_loop(0, 8, products, 0)
    for c in late:
        c.wait()


def near_field(info, src, cnt, charges, mat, fmat, tb, ld):
    v = pl.BlockSpec(memory_space=VMEM)
    s = pl.BlockSpec(memory_space=pltpu.SMEM)
    mats, leaf = VMEM((64, 8, R, R), BF), VMEM((64, R, R), BF)
    return pl.pallas_call(
        near_kernel,
        in_specs=[s] * 3 + [pl.BlockSpec(memory_space=pl.ANY)] * 7,
        out_specs=[v] * 4,
        out_shape=[VMEM((64, R, R), F32), mats, leaf, leaf],
        scratch_shapes=[
            VMEM((96, R, 2 * R), BF),
            mats,
            leaf,
            VMEM((3, R, 2 * R), BF),
            pltpu.SemaphoreType.DMA((21,)),
        ],
        compiler_params=pltpu.CompilerParams(vmem_limit_bytes=BIG),
        cost_estimate=pl.CostEstimate(flops=576 * 2 * R**3, bytes_accessed=24 << 20, transcendentals=0),
        name="near",
    )(info, src, cnt, *charges, mat, fmat, tb, ld)


def far_kernel(info, src, ku, ko, kd, mv, tbv, near, base, table, far, mask, sem):
    tables = copies_of([(ku, table.at[0:32]), (ko, table.at[32:64]), (kd, table.at[64:96])], sem)
    half_masks(mask)
    for c in tables:
        c.wait()

    def leaf(c, carry):
        for g in range(2):
            accs = []
            for j in range(4):
                l = c * 8 + g * 4 + j
                acc = jnp.zeros((R, 2 * R), F32)
                for n in range(8):
                    k = jnp.clip(src[n, l] - info[0], 0, 191)
                    acc += dot(mv[l, n], table[k >> 1] * mask[k & 1])
                accs.append(acc)
            for j in range(4):
                far[c * 8 + g * 4 + j] = fold(accs[j]).astype(BF)
        return carry

    lax.fori_loop(0, 8, leaf, 0)

    def last(i, carry):
        res = [near[8 * i + j] + dot(tbv[8 * i + j], far[8 * i + j]) for j in range(8)]
        for j in range(8):
            base[8 * i + j] = res[j]
        return carry

    lax.fori_loop(0, 8, last, 0)


def leaf_far(info, src, coefs, mat, tb, near):
    v = pl.BlockSpec(memory_space=VMEM)
    s = pl.BlockSpec(memory_space=pltpu.SMEM)
    return pl.pallas_call(
        far_kernel,
        in_specs=[s] * 2 + [pl.BlockSpec(memory_space=pl.ANY)] * 3 + [v] * 3,
        out_specs=v,
        out_shape=VMEM((64, R, R), F32),
        scratch_shapes=[
            VMEM((96, R, 2 * R), BF),
            VMEM((64, R, R), BF),
            VMEM((3, R, 2 * R), BF),
            pltpu.SemaphoreType.DMA((3,)),
        ],
        compiler_params=pltpu.CompilerParams(vmem_limit_bytes=32 << 20),
        cost_estimate=pl.CostEstimate(flops=576 * 2 * R**3, bytes_accessed=16 << 20, transcendentals=0),
        name="leaf_far",
    )(info, src, *coefs, mat, tb, near)


def pick_kernel(*refs):
    rings, out, sem = refs[:16], refs[16], refs[17]
    pairs = []
    for s in range(8):
        for h in range(2):
            for k in range(2):
                q = 4 * s + 2 * h + k
                pairs.append((rings[2 * s + h].at[pl.ds(288 * k + 256, 32)], out.at[pl.ds(32 * q, 32)]))
    for c in copies_of(pairs, sem):
        c.wait()


def pick_tops(rings):
    return pl.pallas_call(
        pick_kernel,
        in_specs=[pl.BlockSpec(memory_space=pl.ANY)] * 16,
        out_specs=pl.BlockSpec(memory_space=VMEM),
        out_shape=VMEM((1024, 128), BF),
        scratch_shapes=[pltpu.SemaphoreType.DMA((32,))],
        compiler_params=pltpu.CompilerParams(vmem_limit_bytes=SMALL),
        cost_estimate=pl.CostEstimate(flops=0, bytes_accessed=1 << 20, transcendentals=0),
        name="pick_tops",
    )(*rings)


def join_kernel(a, b, c, d, out, sem):
    n = a.shape[0]
    for copy in copies_of([(r, out.at[pl.ds(k * n, n)]) for k, r in enumerate((a, b, c, d))], sem):
        copy.wait()


def join(arrays):
    return pl.pallas_call(
        join_kernel,
        in_specs=[pl.BlockSpec(memory_space=pl.ANY)] * 4,
        out_specs=pl.BlockSpec(memory_space=VMEM),
        out_shape=VMEM((4096, 128), BF),
        scratch_shapes=[pltpu.SemaphoreType.DMA((4,))],
        compiler_params=pltpu.CompilerParams(vmem_limit_bytes=SMALL),
        cost_estimate=pl.CostEstimate(flops=0, bytes_accessed=2 << 20, transcendentals=0),
        name="join",
    )(*arrays)


def top_kernel(info, src, own, other, mat, out):
    x, core, z, y = info[1], info[2], info[3], info[4]
    acc = jnp.zeros((R, R), F32)
    rows = []
    for n in range(32):
        g = jnp.clip(src[0, n], 0, X * CORE * Z * Y - 1)
        sy = (y - g) & 3
        sz = (z - (g >> 2)) & 7
        sx = (x - (g >> 6)) & 3
        same = ((g >> 5) & 1) == core
        at = pl.ds(pl.multiple_of(((sx * Z + sz) * Y + sy) * 32, 32), 32)
        t = jnp.where(same, own[at, :], other[at, :])
        rows += [t[:, :R], t[:, R:]]
    for q in range(8):
        acc += dot(wide([mat[0, 4 * q + n] for n in range(4)]), jnp.concatenate(rows[8 * q : 8 * q + 8], axis=0))
    out[...] = acc.astype(BF)


def top_far(info, src, own, other, mat):
    v = pl.BlockSpec(memory_space=VMEM)
    s = pl.BlockSpec(memory_space=pltpu.SMEM)
    return pl.pallas_call(
        top_kernel,
        in_specs=[s, s, v, v, v],
        out_specs=v,
        out_shape=jax.ShapeDtypeStruct((R, R), BF),
        compiler_params=pltpu.CompilerParams(vmem_limit_bytes=SMALL),
        cost_estimate=pl.CostEstimate(flops=32 * 2 * R**3, bytes_accessed=3 << 20, transcendentals=0),
        name="top_far",
    )(info, src, own, other, mat)


def mid_kernel(info, src, mat, *refs):
    rings, (out, raw, mv, mask, sem) = refs[:16], refs[16:]
    z, y = info[3], info[4]
    copies = copies_of([(rings[s], raw.at[s]) for s in range(16)], sem)
    copies += copies_of(parts(mat, mv, 8), sem.at[pl.ds(16, 8)])
    half_masks(mask)
    for c in copies:
        c.wait()
    done = []
    for p in range(8):
        acc = jnp.zeros((R, 2 * R), F32)
        for n in range(16):
            g = jnp.clip(src[p, n] - info[5], 0, Z * Y * 8 - 1)
            sy = (y - (g >> 3)) & 3
            sz = (z - (g >> 5)) & 7
            at = (sy & 1) * 288 + ((g >> 1) & 3) * R
            t = raw[sz * 2 + (sy >> 1), pl.ds(pl.multiple_of(at, 32), R), :]
            acc += dot(mv[p, n], t * mask[g & 1])
        done.append(fold(acc))
    for p in range(8):
        out[p] = done[p]


def mid_far(info, src, mat, rings):
    v = pl.BlockSpec(memory_space=VMEM)
    s = pl.BlockSpec(memory_space=pltpu.SMEM)
    return pl.pallas_call(
        mid_kernel,
        in_specs=[s, s] + [pl.BlockSpec(memory_space=pl.ANY)] * 17,
        out_specs=v,
        out_shape=VMEM((8, R, R), F32),
        scratch_shapes=[
            VMEM((16, 576, 128), BF), VMEM(mat.shape, BF), VMEM((3, R, 2 * R), BF), pltpu.SemaphoreType.DMA((24,)),
        ],
        compiler_params=pltpu.CompilerParams(vmem_limit_bytes=12 << 20),
        cost_estimate=pl.CostEstimate(flops=128 * 2 * R**3, bytes_accessed=6 << 20, transcendentals=0),
        name="mid_far",
    )(info, src, mat, *rings)


def tail_kernel(top_ref, far, down, base, both, out, buf, sem):
    top = top_ref[...]
    local = [(far[p] + dot(down[p], top)).astype(BF) for p in range(8)]
    copies = []
    for p in range(8):
        at = pl.ds(8 * p, 8)
        res = dot(both[at].reshape(8 * R, R), local[p]).reshape(8, R, R)
        buf[at] = (base[at] + res).astype(BF)
        copies.append(pltpu.make_async_copy(buf.at[at], out.at[at], sem.at[p]))
        copies[-1].start()
    for c in copies:
        c.wait()


def tail(top, far, down, base, both):
    v = pl.BlockSpec(memory_space=VMEM)
    return pl.pallas_call(
        tail_kernel,
        in_specs=[v] * 5,
        out_specs=pl.BlockSpec(memory_space=pltpu.HBM),
        out_shape=jax.ShapeDtypeStruct((64, R, R), BF),
        scratch_shapes=[VMEM((64, R, R), BF), pltpu.SemaphoreType.DMA((8,))],
        compiler_params=pltpu.CompilerParams(vmem_limit_bytes=SMALL),
        cost_estimate=pl.CostEstimate(flops=72 * 2 * R**3, bytes_accessed=6 << 20, transcendentals=0),
        name="tail",
    )(top, far, down, base, both)


def place(d):
    return d // (CORE * Z * Y), d // (Z * Y) % CORE, d // Y % Z, d % Y


def index(x, c, z, y):
    return ((x % X * CORE + c % CORE) * Z + z % Z) * Y + y % Y


def shift(a, x=0, c=0, z=0, y=0):
    pairs = []
    for d in range(X * CORE * Z * Y):
        px, pc, pz, py = place(d)
        pairs.append((d, index(px + x, pc + c, pz + z, py + y)))
    return lax.ppermute(a, BOTH, pairs)


def some(a, pairs):
    return lax.ppermute(a, BOTH, pairs)


def halo(a):
    n = X * CORE * Z * Y
    up = [(i, i + 1) for i in range(n - 1)]
    return some(a, up), some(a, [(j, i) for i, j in up])


def tie(*arrays):
    return lax.optimization_barrier(arrays)


def shards(
    charges,
    source_basis,
    target_basis,
    leaf_up,
    mid_up,
    leaf_down,
    mid_down,
    leaf_far_src,
    leaf_far_mat,
    mid_far_src,
    mid_far_mat,
    top_far_src,
    top_far_mat,
    near_src,
    near_count,
    near_mat,
):
    me = lax.axis_index(BOTH).astype(jnp.int32)
    px, pc, pz, py = place(me)
    info = jnp.stack([(me - 1) * 64, px, pc, pz, py, me // (Z * Y) * (Z * Y * 8)])

    packed, coef, mt = upsweep(charges, source_basis, leaf_up, mid_up)

    m1, m3, m2 = shift(mt, y=1), shift(mt, y=-1), shift(mt, y=2)
    rings = {(0, 0): jnp.concatenate([mt, m1], axis=0), (0, 1): jnp.concatenate([m2, m3], axis=0)}
    for s in range(1, 4):
        for h in range(2):
            rings[s, h] = shift(rings[s - 1, h], z=1)
            rings[8 - s, h] = shift(rings[(9 - s) % 8, h], z=-1)
    rings[4, 0] = shift(rings[3, 0], z=1)
    rings[4, 1] = shift(rings[5, 1], z=-1)
    rings = [rings[s, h] for s in range(8) for h in range(2)]

    all_z = pick_tops(rings)
    all_z, rings[0], packed, coef = tie(all_z, rings[0], packed, coef)
    by_x = [all_z] + [shift(all_z, x=s) for s in range(1, X)]
    before, after = halo(packed)
    far = mid_far(info, mid_far_src, mid_far_mat, rings)
    packed, far = tie(packed, far)
    coef_before, coef_after = halo(coef)
    near, far_v, tb_v, both = near_field(
        info, near_src.T, near_count, (before, packed, after), near_mat, leaf_far_mat, target_basis, leaf_down
    )
    by_x[1], near, coef_before, coef_after = tie(by_x[1], near, coef_before, coef_after)
    all_x = join(by_x)
    other = shift(all_x, c=1)
    base = leaf_far(info, leaf_far_src.T, (coef_before, coef, coef_after), far_v, tb_v, near)
    top_local = top_far(info, top_far_src, all_x, other, top_far_mat)
    return tail(top_local, far, mid_down, base, both)


def solution(mesh):
    row = P(BOTH, None)
    three = P(BOTH, None, None)
    four = P(BOTH, None, None, None)
    in_specs = (
        three, three, three, three, three, three, three,
        row, four, row, four, row, four, row, P(BOTH), four,
    )
    return jax.shard_map(shards, mesh=mesh, in_specs=in_specs, out_specs=three, check_vma=False)
```
